32 devices in a mesh: scale: 8 (over y, x, core), rt: 4 (over z).
Axes of the slice: x: 2, y: 2, z: 4, core: 2. Of those that a mesh axis runs over, the one named last changes fastest.
Arguments:
- slab: float32 [96, 128, 896], P('rt'), may hold values from -6 to 6
- widths: int32 [8], replicated, may hold values from 1 to 8
Outputs:
- peak: bfloat16 [96, 128, 896], P('rt', 'scale')
- energy: float32 [96, 128, 896], P('rt', 'scale')
The draws below stay inside these ranges and needn't reach their ends.
All inputs are finite; a program needn't handle non-finite values.
Results may differ from the reference program's by a relative error of at most 0.006.
Values may be sent and summed in bfloat16 or wider, within the bound.
A program may use at most 128 MiB of HBM per device.

```python
import jax
import jax.numpy as jnp
from jax import lax

MZ = 128
SCANS = 896
SCAN_RATIO = 16
HALO = 24
WMAX = 8
FRAMES = 96
SCALES = 8


def plant(result, rng, smallest, high):
    dims = result.shape
    spot = [jax.random.randint(jax.random.fold_in(rng, axis), (), 0, dims[axis]) for axis in range(len(dims))]
    result = result.at[tuple(spot)].set(smallest)
    longest = dims.index(max(dims))
    spot[longest] = (spot[longest] + 1) % dims[longest]
    return result.at[tuple(spot)].set(high)


def steps_of(rng, dims, pieces, smallest, largest):
    level, own = 1.0, jax.random.fold_in(rng, 6)
    for position, blocks in pieces:
        steps = jnp.exp(jax.random.uniform(jax.random.fold_in(own, position), (blocks,), jnp.float32, smallest / len(pieces), largest / len(pieces)))
        level = level * jnp.repeat(steps, dims[position] // blocks).reshape([-1 if axis == position else 1 for axis in range(len(dims))])
    return level


def centred(rng, extent, scale, bound, shards=(), kind=jnp.bfloat16):
    result = jax.random.normal(rng, extent, jnp.float32) * scale
    if len(shards) > 0:
        result = steps_of(rng, extent, shards, -0.22, 0.18) * result
    return jnp.clip(result, min=-bound, max=bound).astype(kind)


def setup_inputs(seed: int = 0) -> dict:
    streams_of = jax.random.split(jax.random.key(seed), 3)
    slab = centred(streams_of[0], (FRAMES, MZ, SCANS), 1.0, 6.0, ((0, 4),), jnp.float32)
    widths = plant(jax.random.randint(streams_of[1], (SCALES,), 1, WMAX + 1), jax.random.fold_in(streams_of[1], 1), 1, WMAX).astype(jnp.int32)
    return dict(slab=slab, widths=widths)


def mexican(offsets, spread):
    ratio = offsets / spread
    return (1.0 - ratio * ratio) * jnp.exp(-0.5 * ratio * ratio) / jnp.sqrt(spread)

def to_bf16_and_back(values):
    return lax.optimization_barrier(values.astype(jnp.bfloat16)).astype(jnp.float32)

def reference(slab, widths):
    signal = to_bf16_and_back(slab)
    scan_pos = jnp.arange(SCANS, dtype=jnp.float32)
    scan_diff = scan_pos[:, None] - scan_pos[None, :]
    frame_pos = jnp.arange(FRAMES, dtype=jnp.float32)
    frame_diff = frame_pos[None, :] - frame_pos[:, None]
    inside = jnp.abs(frame_diff) <= HALO

    def one_scale(carry, width_value):
        best, total = carry
        scale_width = width_value.astype(jnp.float32)
        scan_table = to_bf16_and_back(mexican(scan_diff, SCAN_RATIO * scale_width))
        frame_table = to_bf16_and_back(jnp.where(inside, mexican(frame_diff, scale_width), 0.0))
        smooth = jnp.einsum('fms,st->fmt', signal, scan_table, precision=lax.Precision.HIGHEST)
        smooth = to_bf16_and_back(smooth)
        answer = jnp.einsum('fj,jmt->fmt', frame_table, smooth, precision=lax.Precision.HIGHEST)
        answer = to_bf16_and_back(answer)
        return ((jnp.maximum(best, answer), total + answer * answer), None)
    start = (jnp.full(slab.shape, -jnp.inf, jnp.float32), jnp.zeros(slab.shape, jnp.float32))
    (best, total), _ = lax.scan(one_scale, start, widths)
    return (best.astype(jnp.bfloat16), total)
```

```python
import functools

import jax
import jax.numpy as jnp
from jax import lax
from jax.experimental import pallas as pl
from jax.experimental.pallas import tpu as pltpu
from jax.sharding import PartitionSpec as P

SCAN_RATIO = 16
LANES = 128
GROUPS = 2
MESH = pl.DeviceIdType.MESH


def mexican(ratio, spread):
    square = ratio * ratio
    return (1.0 - square) * jnp.exp(-0.5 * square) * lax.rsqrt(spread)


def frame_tables(widths_ref, ftab, scales, frames):
    shape = (2 * frames, 6 * frames)
    row = lax.broadcasted_iota(jnp.int32, shape, 0)
    col = lax.broadcasted_iota(jnp.int32, shape, 1)
    row_bin = (row >= frames).astype(jnp.int32)
    part = (col >= 2 * frames).astype(jnp.int32) + (col >= 4 * frames).astype(jnp.int32)
    rest = col - part * (2 * frames)
    col_bin = (rest >= frames).astype(jnp.int32)
    offset = (rest - col_bin * frames) + (part - 1) * frames - (row - row_bin * frames)
    keep = (row_bin == col_bin) & (jnp.abs(offset) <= frames)
    offset = offset.astype(jnp.float32)
    for scale in range(scales):
        spread = jnp.full(shape, widths_ref[scale].astype(jnp.float32))
        values = mexican(offset / spread, spread)
        ftab[pl.ds(scale * 2 * frames, 2 * frames), :] = jnp.where(keep, values, 0.0).astype(
            jnp.bfloat16
        )


def scan_tables(widths_ref, hats, scales, scans):
    span = hats.shape[2]

    def one(scale, carry):
        spread = jnp.full((LANES, LANES), SCAN_RATIO * widths_ref[scale].astype(jnp.float32))
        inverse = 1.0 / spread
        root = lax.rsqrt(spread)
        base = lax.broadcasted_iota(jnp.int32, (LANES, LANES), 0) - lax.broadcasted_iota(
            jnp.int32, (LANES, LANES), 1
        )
        for tile in range(span // LANES):
            offset = (base + (scans - LANES - tile * LANES)).astype(jnp.float32)
            ratio = offset * inverse
            square = ratio * ratio
            values = (1.0 - square) * jnp.exp(-0.5 * square) * root
            hats[scale, :, tile * LANES : (tile + 1) * LANES] = values.astype(jnp.bfloat16)
        return carry

    lax.fori_loop(0, scales, one, 0)


def kernel(
    rt_count,
    widths_ref,
    slab_ref,
    peak_ref,
    energy_ref,
    raw,
    block,
    ftab,
    hats,
    smooth,
    total,
    best,
    power,
    best_out,
    best_half,
    power_out,
    in_sem,
    send_sem,
    recv_sem,
    out_sem,
):
    tiles, frames, strip, _ = raw.shape
    scales, rows, scans = total.shape
    pairs = strip // 2
    twice = 2 * frames
    me = lax.axis_index("rt")
    first_bin = pl.multiple_of(lax.axis_index("scale") * strip, strip)

    loads = []
    for tile in range(tiles):
        load = pltpu.make_async_copy(
            slab_ref.at[:, pl.ds(first_bin, strip), pl.ds(tile * LANES, LANES)],
            raw.at[tile],
            in_sem.at[tile],
        )
        load.start()
        loads.append(load)

    barrier = pltpu.get_barrier_semaphore()
    has_low, has_high = me > 0, me < rt_count - 1

    @pl.when(has_low)
    def _():
        pl.semaphore_signal(barrier, inc=1, device_id={"rt": me - 1}, device_id_type=MESH)

    @pl.when(has_high)
    def _():
        pl.semaphore_signal(barrier, inc=1, device_id={"rt": me + 1}, device_id_type=MESH)

    has_both = has_low & has_high

    @pl.when(has_both)
    def _():
        pl.semaphore_wait(barrier, 2)

    @pl.when(jnp.logical_not(has_both))
    def _():
        pl.semaphore_wait(barrier, 1)

    def copies(tile):
        own = block.at[tile, :, pl.ds(twice, twice), :]
        up = pltpu.make_async_remote_copy(
            src_ref=own,
            dst_ref=block.at[tile, :, pl.ds(0, twice), :],
            send_sem=send_sem.at[0, tile],
            recv_sem=recv_sem.at[0, tile],
            device_id={"rt": me + 1},
            device_id_type=MESH,
        )
        down = pltpu.make_async_remote_copy(
            src_ref=own,
            dst_ref=block.at[tile, :, pl.ds(2 * twice, twice), :],
            send_sem=send_sem.at[1, tile],
            recv_sem=recv_sem.at[1, tile],
            device_id={"rt": me - 1},
            device_id_type=MESH,
        )
        return up, down

    flat = raw.reshape(tiles * frames * strip, LANES)
    for tile in range(tiles):
        loads[tile].wait()
        for pair in range(pairs):
            parts = [
                flat[pl.ds(tile * frames * strip + 2 * pair + half, frames, stride=strip), :]
                for half in range(2)
            ]
            block[tile, pair, twice : 2 * twice, :] = jnp.concatenate(parts, axis=0).astype(
                jnp.bfloat16
            )
        up, down = copies(tile)
        pl.when(has_high)(up.start)
        pl.when(has_low)(down.start)

    @pl.when(jnp.logical_not(has_low))
    def _():
        block[:, :, 0:twice, :] = jnp.zeros((tiles, pairs, twice, LANES), jnp.bfloat16)

    @pl.when(jnp.logical_not(has_high))
    def _():
        block[:, :, 2 * twice : 3 * twice, :] = jnp.zeros(
            (tiles, pairs, twice, LANES), jnp.bfloat16
        )

    frame_tables(widths_ref, ftab, scales, frames)
    scan_tables(widths_ref, hats, scales, scans)

    starts = list(range(0, tiles, GROUPS))
    for start in starts:
        group = list(range(start, min(start + GROUPS, tiles)))
        depth = len(group) * LANES
        for tile in group:
            up, down = copies(tile)
            pl.when(has_low)(up.wait_recv)
            pl.when(has_high)(down.wait_recv)

        def frame_step(pair, carry):
            data = jnp.concatenate([block[tile, pair] for tile in group], axis=1)
            mixed = jnp.dot(ftab[...], data, preferred_element_type=jnp.float32)
            mixed = mixed.astype(jnp.bfloat16).reshape(scales, twice, depth)
            smooth[:, pl.ds(pl.multiple_of(pair * twice, twice), twice), 0:depth] = mixed
            return carry

        lax.fori_loop(0, pairs, frame_step, 0)

        def scan_step(scale, carry):
            table = jnp.concatenate(
                [
                    hats[scale, :, scans - LANES * (tile + 1) : 2 * scans - LANES * (tile + 1)]
                    for tile in group
                ],
                axis=0,
            )
            part = jnp.dot(
                smooth[scale, :, 0:depth], table, preferred_element_type=jnp.float32
            )
            if start > 0:
                part = part + total[scale]
            if start != starts[-1]:
                total[scale] = part
            else:
                best[...] = jnp.maximum(best[...], part)
                power[...] = power[...] + part * part
            return carry

        if start == starts[-1]:
            best[...] = jnp.full(best.shape, -jnp.inf, jnp.float32)
            power[...] = jnp.zeros(power.shape, jnp.float32)
        lax.fori_loop(0, scales, scan_step, 0)

    best_flat = best_out.reshape(tiles * frames * strip, LANES)
    power_flat = power_out.reshape(tiles * frames * strip, LANES)
    stores = []
    for tile in range(tiles):
        lanes = pl.ds(tile * LANES, LANES)
        for mz in range(strip):
            where = pl.ds(tile * frames * strip + mz, frames, stride=strip)
            best_flat[where, :] = best[mz * frames : (mz + 1) * frames, lanes]
            power_flat[where, :] = power[mz * frames : (mz + 1) * frames, lanes]
        best_half[tile] = best_out[tile].astype(jnp.bfloat16)
        for slot, (source, target) in enumerate(((best_half, peak_ref), (power_out, energy_ref))):
            store = pltpu.make_async_copy(
                source.at[tile], target.at[:, :, lanes], out_sem.at[slot, tile]
            )
            store.start()
            stores.append(store)
    for tile in range(tiles):
        up, down = copies(tile)
        pl.when(has_high)(up.wait_send)
        pl.when(has_low)(down.wait_send)
    for store in stores:
        store.wait()


def per_device(slab, widths):
    frames, mz_bins, scans = slab.shape
    scales = widths.shape[0]
    strip = mz_bins // lax.axis_size("scale")
    tiles = scans // LANES
    rows = frames * strip
    bf16, f32 = jnp.bfloat16, jnp.float32
    flops = 2 * scales * rows * scans * (scans + 6 * frames)
    return pl.pallas_call(
        functools.partial(kernel, lax.axis_size("rt")),
        out_shape=(
            jax.ShapeDtypeStruct((frames, strip, scans), bf16),
            jax.ShapeDtypeStruct((frames, strip, scans), f32),
        ),
        in_specs=[
            pl.BlockSpec(memory_space=pltpu.SMEM),
            pl.BlockSpec(memory_space=pl.ANY),
        ],
        out_specs=(pl.BlockSpec(memory_space=pl.ANY), pl.BlockSpec(memory_space=pl.ANY)),
        scratch_shapes=[
            pltpu.VMEM((tiles, frames, strip, LANES), f32),
            pltpu.VMEM((tiles, strip // 2, 6 * frames, LANES), bf16),
            pltpu.VMEM((scales * 2 * frames, 6 * frames), bf16),
            pltpu.VMEM((scales, LANES, 2 * scans - LANES), bf16),
            pltpu.VMEM((scales, rows, GROUPS * LANES), bf16),
            pltpu.VMEM((scales, rows, scans), f32),
            pltpu.VMEM((rows, scans), f32),
            pltpu.VMEM((rows, scans), f32),
            pltpu.VMEM((tiles, frames, strip, LANES), f32),
            pltpu.VMEM((tiles, frames, strip, LANES), bf16),
            pltpu.VMEM((tiles, frames, strip, LANES), f32),
            pltpu.SemaphoreType.DMA((tiles,)),
            pltpu.SemaphoreType.DMA((2, tiles)),
            pltpu.SemaphoreType.DMA((2, tiles)),
            pltpu.SemaphoreType.DMA((2, tiles)),
        ],
        compiler_params=pltpu.CompilerParams(
            collective_id=0, has_side_effects=True, vmem_limit_bytes=58 * 1024 * 1024
        ),
        cost_estimate=pl.CostEstimate(
            flops=flops, bytes_accessed=10 * rows * scans, transcendentals=0
        ),
        name="wavelets",
    )(widths, slab)


def solution(mesh):
    in_specs = (P("rt", None, None), P())
    out_specs = (P("rt", "scale", None), P("rt", "scale", None))
    return jax.shard_map(
        per_device, mesh=mesh, in_specs=in_specs, out_specs=out_specs, check_vma=False
    )
```

```python
import functools

import jax
import jax.numpy as jnp
from jax import lax
from jax.experimental import pallas as pl
from jax.experimental.pallas import tpu as pltpu
from jax.sharding import PartitionSpec as P

SCAN_RATIO = 16
LANES = 128
EDGES = (4,)
COLUMNS = 256
FRAME_UNROLL = 8
LEAD = 4
SCAN_UNROLL = 8
MESH = pl.DeviceIdType.MESH


def mexican(ratio, spread):
    square = ratio * ratio
    return (1.0 - square) * jnp.exp(-0.5 * square) * lax.rsqrt(spread)


def frame_tables(widths_ref, ftab, scales, frames):
    shape = (2 * frames, 6 * frames)
    row = lax.broadcasted_iota(jnp.int32, shape, 0)
    col = lax.broadcasted_iota(jnp.int32, shape, 1)
    row_bin = (row >= frames).astype(jnp.int32)
    part = (col >= 2 * frames).astype(jnp.int32) + (col >= 4 * frames).astype(jnp.int32)
    rest = col - part * (2 * frames)
    col_bin = (rest >= frames).astype(jnp.int32)
    offset = (rest - col_bin * frames) + (part - 1) * frames - (row - row_bin * frames)
    keep = (row_bin == col_bin) & (jnp.abs(offset) <= frames)
    offset = offset.astype(jnp.float32)
    for scale in range(scales):
        spread = jnp.full(shape, widths_ref[scale].astype(jnp.float32))
        values = mexican(offset / spread, spread)
        ftab[pl.ds(scale * 2 * frames, 2 * frames), :] = jnp.where(keep, values, 0.0).astype(
            jnp.bfloat16
        )


def scan_tables(widths_ref, hats, scales, scans):
    span = hats.shape[2]

    def one(scale, carry):
        spread = jnp.full((LANES, LANES), SCAN_RATIO * widths_ref[scale].astype(jnp.float32))
        inverse = 1.0 / spread
        root = lax.rsqrt(spread)
        base = lax.broadcasted_iota(jnp.int32, (LANES, LANES), 0) - lax.broadcasted_iota(
            jnp.int32, (LANES, LANES), 1
        )
        for tile in range(span // LANES):
            offset = (base + (scans - LANES - tile * LANES)).astype(jnp.float32)
            ratio = offset * inverse
            square = ratio * ratio
            values = (1.0 - square) * jnp.exp(-0.5 * square) * root
            hats[scale, :, tile * LANES : (tile + 1) * LANES] = values.astype(jnp.bfloat16)
        return carry

    lax.fori_loop(0, scales, one, 0)


def kernel(
    rt_count,
    widths_ref,
    slab_ref,
    peak_ref,
    energy_ref,
    raw,
    block,
    ftab,
    hats,
    smooth,
    total,
    best,
    power,
    best_out,
    best_half,
    power_out,
    in_sem,
    send_sem,
    recv_sem,
    out_sem,
):
    tiles, frames, strip, _ = raw.shape
    scales, rows, scans = total.shape
    pairs = strip // 2
    twice = 2 * frames
    me = lax.axis_index("rt")
    first_bin = pl.multiple_of(lax.axis_index("scale") * strip, strip)

    loads = []
    for tile in range(tiles):
        load = pltpu.make_async_copy(
            slab_ref.at[:, pl.ds(first_bin, strip), pl.ds(tile * LANES, LANES)],
            raw.at[tile],
            in_sem.at[tile],
        )
        load.start()
        loads.append(load)

    barrier = pltpu.get_barrier_semaphore()
    has_low, has_high = me > 0, me < rt_count - 1

    @pl.when(has_low)
    def _():
        pl.semaphore_signal(barrier, inc=1, device_id={"rt": me - 1}, device_id_type=MESH)

    @pl.when(has_high)
    def _():
        pl.semaphore_signal(barrier, inc=1, device_id={"rt": me + 1}, device_id_type=MESH)

    has_both = has_low & has_high

    @pl.when(has_both)
    def _():
        pl.semaphore_wait(barrier, 2)

    @pl.when(jnp.logical_not(has_both))
    def _():
        pl.semaphore_wait(barrier, 1)

    def copies(tile):
        own = block.at[tile, :, pl.ds(twice, twice), :]
        up = pltpu.make_async_remote_copy(
            src_ref=own,
            dst_ref=block.at[tile, :, pl.ds(0, twice), :],
            send_sem=send_sem.at[0, tile],
            recv_sem=recv_sem.at[0, tile],
            device_id={"rt": me + 1},
            device_id_type=MESH,
        )
        down = pltpu.make_async_remote_copy(
            src_ref=own,
            dst_ref=block.at[tile, :, pl.ds(2 * twice, twice), :],
            send_sem=send_sem.at[1, tile],
            recv_sem=recv_sem.at[1, tile],
            device_id={"rt": me - 1},
            device_id_type=MESH,
        )
        return up, down

    def send(tile):
        up, down = copies(tile)
        pl.when(has_high)(up.start)
        pl.when(has_low)(down.start)

    flat = raw.reshape(tiles * frames * strip, LANES)
    for tile in range(tiles):
        loads[tile].wait()
        for pair in range(pairs):
            parts = [
                flat[pl.ds(tile * frames * strip + 2 * pair + half, frames, stride=strip), :]
                for half in range(2)
            ]
            block[tile, pair, twice : 2 * twice, :] = jnp.concatenate(parts, axis=0).astype(
                jnp.bfloat16
            )
        if tile < LEAD:
            send(tile)

    @pl.when(jnp.logical_not(has_low))
    def _():
        block[:, :, 0:twice, :] = jnp.zeros((tiles, pairs, twice, LANES), jnp.bfloat16)

    @pl.when(jnp.logical_not(has_high))
    def _():
        block[:, :, 2 * twice : 3 * twice, :] = jnp.zeros(
            (tiles, pairs, twice, LANES), jnp.bfloat16
        )

    frame_tables(widths_ref, ftab, scales, frames)
    scan_tables(widths_ref, hats, scales, scans)

    best_flat = best_out.reshape(tiles * frames * strip, LANES)
    power_flat = power_out.reshape(tiles * frames * strip, LANES)
    stores = []

    def finish(tile):
        lanes = pl.ds(tile * LANES, LANES)
        for mz in range(strip):
            where = pl.ds(tile * frames * strip + mz, frames, stride=strip)
            best_flat[where, :] = best[mz * frames : (mz + 1) * frames, lanes]
            power_flat[where, :] = power[mz * frames : (mz + 1) * frames, lanes]
        best_half[tile] = best_out[tile].astype(jnp.bfloat16)
        for slot, (source, target) in enumerate(((best_half, peak_ref), (power_out, energy_ref))):
            store = pltpu.make_async_copy(
                source.at[tile], target.at[:, :, lanes], out_sem.at[slot, tile]
            )
            store.start()
            stores.append(store)

    def table(scale, group, low, high):
        windows = [scans - LANES * (tile + 1) for tile in group]
        return jnp.concatenate([hats[scale, :, at + low : at + high] for at in windows], axis=0)

    def frame_sums(group, place):
        width = len(group) * LANES
        for tile in group:
            up, down = copies(tile)
            pl.when(has_low)(up.wait_recv)
            pl.when(has_high)(down.wait_recv)
            if tile + LEAD < tiles:
                send(tile + LEAD)

        def step(turn, carry):
            for one in range(FRAME_UNROLL):
                pair = turn * FRAME_UNROLL + one
                data = jnp.concatenate([block[tile, pair] for tile in group], axis=1)
                mixed = jnp.dot(ftab[...], data, preferred_element_type=jnp.float32)
                mixed = mixed.astype(jnp.bfloat16).reshape(scales, twice, width)
                rows_of = pl.ds(pl.multiple_of(pair * twice, twice), twice)
                smooth[:, rows_of, place : place + width] = mixed
            return carry

        lax.fori_loop(0, pairs // FRAME_UNROLL, step, 0)

    splits = [edge for edge in EDGES if edge < tiles] + [tiles]
    columns = [(low, min(low + COLUMNS, scans)) for low in range(0, scans, COLUMNS)]
    begin = 0
    for end in splits:
        group = list(range(begin, end))
        depth = len(group) * LANES
        for at in range(0, len(group), 2):
            frame_sums(group[at : at + 2], at * LANES)
        first, last = begin == 0, end == tiles
        begin = end

        def part_of(scale, low, high):
            part = jnp.dot(
                smooth[scale, :, 0:depth],
                table(scale, group, low, high),
                preferred_element_type=jnp.float32,
            )
            return part if first else part + total[scale, :, low:high]

        if not last:

            def scan_step(scale, carry):
                for low, high in columns:
                    total[scale, :, low:high] = part_of(scale, low, high)
                return carry

            lax.fori_loop(0, scales, scan_step, 0)
            continue
        for low, high in columns:

            def last_step(turn, carry):
                peak, energy = best[:, low:high], power[:, low:high]
                for one in range(SCAN_UNROLL):
                    part = part_of(turn * SCAN_UNROLL + one, low, high)
                    peak = jnp.maximum(peak, part)
                    energy = energy + part * part
                best[:, low:high] = peak
                power[:, low:high] = energy
                return carry

            best[:, low:high] = jnp.full((rows, high - low), -jnp.inf, jnp.float32)
            power[:, low:high] = jnp.zeros((rows, high - low), jnp.float32)
            lax.fori_loop(0, scales // SCAN_UNROLL, last_step, 0)
            for tile in range(low // LANES, high // LANES):
                finish(tile)

    for tile in range(tiles):
        up, down = copies(tile)
        pl.when(has_high)(up.wait_send)
        pl.when(has_low)(down.wait_send)
    for store in stores:
        store.wait()


def per_device(slab, widths):
    frames, mz_bins, scans = slab.shape
    scales = widths.shape[0]
    strip = mz_bins // lax.axis_size("scale")
    tiles = scans // LANES
    rows = frames * strip
    bf16, f32 = jnp.bfloat16, jnp.float32
    edges = [0] + [edge for edge in EDGES if edge < tiles] + [tiles]
    depth = LANES * max(high - low for low, high in zip(edges, edges[1:]))
    flops = 2 * scales * rows * scans * (scans + 6 * frames)
    return pl.pallas_call(
        functools.partial(kernel, lax.axis_size("rt")),
        out_shape=(
            jax.ShapeDtypeStruct((frames, strip, scans), bf16),
            jax.ShapeDtypeStruct((frames, strip, scans), f32),
        ),
        in_specs=[
            pl.BlockSpec(memory_space=pltpu.SMEM),
            pl.BlockSpec(memory_space=pl.ANY),
        ],
        out_specs=(pl.BlockSpec(memory_space=pl.ANY), pl.BlockSpec(memory_space=pl.ANY)),
        scratch_shapes=[
            pltpu.VMEM((tiles, frames, strip, LANES), f32),
            pltpu.VMEM((tiles, strip // 2, 6 * frames, LANES), bf16),
            pltpu.VMEM((scales * 2 * frames, 6 * frames), bf16),
            pltpu.VMEM((scales, LANES, 2 * scans - LANES), bf16),
            pltpu.VMEM((scales, rows, depth), bf16),
            pltpu.VMEM((scales, rows, scans), f32),
            pltpu.VMEM((rows, scans), f32),
            pltpu.VMEM((rows, scans), f32),
            pltpu.VMEM((tiles, frames, strip, LANES), f32),
            pltpu.VMEM((tiles, frames, strip, LANES), bf16),
            pltpu.VMEM((tiles, frames, strip, LANES), f32),
            pltpu.SemaphoreType.DMA((tiles,)),
            pltpu.SemaphoreType.DMA((2, tiles)),
            pltpu.SemaphoreType.DMA((2, tiles)),
            pltpu.SemaphoreType.DMA((2, tiles)),
        ],
        compiler_params=pltpu.CompilerParams(
            collective_id=0, has_side_effects=True, vmem_limit_bytes=58 * 1024 * 1024
        ),
        cost_estimate=pl.CostEstimate(
            flops=flops, bytes_accessed=10 * rows * scans, transcendentals=0
        ),
        name="wavelets",
    )(widths, slab)


def solution(mesh):
    in_specs = (P("rt", None, None), P())
    out_specs = (P("rt", "scale", None), P("rt", "scale", None))
    return jax.shard_map(
        per_device, mesh=mesh, in_specs=in_specs, out_specs=out_specs, check_vma=False
    )
```

```python
import functools

import jax
import jax.numpy as jnp
from jax import lax
from jax.experimental import pallas as pl
from jax.experimental.pallas import tpu as pltpu
from jax.sharding import PartitionSpec as P

SCAN_RATIO = 16
LANES = 128
EDGES = (4,)
COLUMNS = 256
FRAME_UNROLL = 8
LEAD = 4
SCAN_UNROLL = 8
MESH = pl.DeviceIdType.MESH


def mexican(ratio, spread):
    square = ratio * ratio
    return (1.0 - square) * jnp.exp(-0.5 * square) * lax.rsqrt(spread)


def frame_tables(widths_ref, ftab, scales, frames):
    shape = (2 * frames, 6 * frames)
    row = lax.broadcasted_iota(jnp.int32, shape, 0)
    col = lax.broadcasted_iota(jnp.int32, shape, 1)
    row_bin = (row >= frames).astype(jnp.int32)
    part = (col >= 2 * frames).astype(jnp.int32) + (col >= 4 * frames).astype(jnp.int32)
    rest = col - part * (2 * frames)
    col_bin = (rest >= frames).astype(jnp.int32)
    offset = (rest - col_bin * frames) + (part - 1) * frames - (row - row_bin * frames)
    keep = (row_bin == col_bin) & (jnp.abs(offset) <= frames)
    offset = offset.astype(jnp.float32)
    for scale in range(scales):
        spread = jnp.full(shape, widths_ref[scale].astype(jnp.float32))
        values = mexican(offset / spread, spread)
        ftab[pl.ds(scale * 2 * frames, 2 * frames), :] = jnp.where(keep, values, 0.0).astype(
            jnp.bfloat16
        )


def scan_tables(widths_ref, hats, scales, scans):
    span = hats.shape[2]

    def one(scale, carry):
        spread = jnp.full((LANES, LANES), SCAN_RATIO * widths_ref[scale].astype(jnp.float32))
        inverse = 1.0 / spread
        root = lax.rsqrt(spread)
        base = lax.broadcasted_iota(jnp.int32, (LANES, LANES), 0) - lax.broadcasted_iota(
            jnp.int32, (LANES, LANES), 1
        )
        for tile in range(span // LANES):
            offset = (base + (scans - LANES - tile * LANES)).astype(jnp.float32)
            ratio = offset * inverse
            square = ratio * ratio
            values = (1.0 - square) * jnp.exp(-0.5 * square) * root
            hats[scale, :, tile * LANES : (tile + 1) * LANES] = values.astype(jnp.bfloat16)
        return carry

    lax.fori_loop(0, scales, one, 0)


def kernel(
    rt_count,
    widths_ref,
    slab_ref,
    peak_ref,
    energy_ref,
    raw,
    block,
    ftab,
    hats,
    smooth,
    total,
    best,
    power,
    best_out,
    best_half,
    power_out,
    in_sem,
    send_sem,
    recv_sem,
    out_sem,
):
    tiles, frames, strip, _ = raw.shape
    scales, rows, scans = total.shape
    pairs = strip // 2
    twice = 2 * frames
    me = lax.axis_index("rt")
    first_bin = pl.multiple_of(lax.axis_index("scale") * strip, strip)

    loads = []
    for tile in range(tiles):
        load = pltpu.make_async_copy(
            slab_ref.at[:, pl.ds(first_bin, strip), pl.ds(tile * LANES, LANES)],
            raw.at[tile],
            in_sem.at[tile],
        )
        load.start()
        loads.append(load)

    barrier = pltpu.get_barrier_semaphore()
    has_low, has_high = me > 0, me < rt_count - 1

    @pl.when(has_low)
    def _():
        pl.semaphore_signal(barrier, inc=1, device_id={"rt": me - 1}, device_id_type=MESH)

    @pl.when(has_high)
    def _():
        pl.semaphore_signal(barrier, inc=1, device_id={"rt": me + 1}, device_id_type=MESH)

    has_both = has_low & has_high

    @pl.when(has_both)
    def _():
        pl.semaphore_wait(barrier, 2)

    @pl.when(jnp.logical_not(has_both))
    def _():
        pl.semaphore_wait(barrier, 1)

    def copies(tile):
        own = block.at[tile, :, pl.ds(twice, twice), :]
        up = pltpu.make_async_remote_copy(
            src_ref=own,
            dst_ref=block.at[tile, :, pl.ds(0, twice), :],
            send_sem=send_sem.at[0, tile],
            recv_sem=recv_sem.at[0, tile],
            device_id={"rt": me + 1},
            device_id_type=MESH,
        )
        down = pltpu.make_async_remote_copy(
            src_ref=own,
            dst_ref=block.at[tile, :, pl.ds(2 * twice, twice), :],
            send_sem=send_sem.at[1, tile],
            recv_sem=recv_sem.at[1, tile],
            device_id={"rt": me - 1},
            device_id_type=MESH,
        )
        return up, down

    def send(tile):
        up, down = copies(tile)
        pl.when(has_high)(up.start)
        pl.when(has_low)(down.start)

    flat = raw.reshape(tiles * frames * strip, LANES)
    for tile in range(tiles):
        loads[tile].wait()
        for pair in range(pairs):
            parts = [
                flat[pl.ds(tile * frames * strip + 2 * pair + half, frames, stride=strip), :]
                for half in range(2)
            ]
            block[tile, pair, twice : 2 * twice, :] = jnp.concatenate(parts, axis=0).astype(
                jnp.bfloat16
            )
        if tile < LEAD:
            send(tile)

    @pl.when(jnp.logical_not(has_low))
    def _():
        block[:, :, 0:twice, :] = jnp.zeros((tiles, pairs, twice, LANES), jnp.bfloat16)

    @pl.when(jnp.logical_not(has_high))
    def _():
        block[:, :, 2 * twice : 3 * twice, :] = jnp.zeros(
            (tiles, pairs, twice, LANES), jnp.bfloat16
        )

    frame_tables(widths_ref, ftab, scales, frames)
    scan_tables(widths_ref, hats, scales, scans)

    best_flat = best_out.reshape(tiles * frames * strip, LANES)
    power_flat = power_out.reshape(tiles * frames * strip, LANES)
    stores = []

    def finish(tile):
        lanes = pl.ds(tile * LANES, LANES)
        for mz in range(strip):
            where = pl.ds(tile * frames * strip + mz, frames, stride=strip)
            best_flat[where, :] = best[mz * frames : (mz + 1) * frames, lanes]
            power_flat[where, :] = power[mz * frames : (mz + 1) * frames, lanes]
        best_half[tile] = best_out[tile].astype(jnp.bfloat16)
        for slot, (source, target) in enumerate(((best_half, peak_ref), (power_out, energy_ref))):
            store = pltpu.make_async_copy(
                source.at[tile], target.at[:, :, lanes], out_sem.at[slot, tile]
            )
            store.start()
            stores.append(store)

    def table(scale, group, low, high):
        windows = [scans - LANES * (tile + 1) for tile in group]
        return jnp.concatenate([hats[scale, :, at + low : at + high] for at in windows], axis=0)

    def frame_sums(group, place):
        width = len(group) * LANES
        for tile in group:
            up, down = copies(tile)
            pl.when(has_low)(up.wait_recv)
            pl.when(has_high)(down.wait_recv)
            if tile + LEAD < tiles:
                send(tile + LEAD)

        def step(turn, carry):
            for one in range(FRAME_UNROLL):
                pair = turn * FRAME_UNROLL + one
                data = jnp.concatenate([block[tile, pair] for tile in group], axis=1)
                mixed = jnp.dot(ftab[...], data, preferred_element_type=jnp.float32)
                mixed = mixed.astype(jnp.bfloat16).reshape(scales, twice, width)
                rows_of = pl.ds(pl.multiple_of(pair * twice, twice), twice)
                smooth[:, rows_of, place : place + width] = mixed
            return carry

        lax.fori_loop(0, pairs // FRAME_UNROLL, step, 0)

    splits = [edge for edge in EDGES if edge < tiles] + [tiles]
    columns = [(low, min(low + COLUMNS, scans)) for low in range(0, scans, COLUMNS)]
    begin = 0
    for end in splits:
        group = list(range(begin, end))
        depth = len(group) * LANES
        for at in range(0, len(group), 2):
            frame_sums(group[at : at + 2], at * LANES)
        first, last = begin == 0, end == tiles
        begin = end

        def part_of(scale, low, high):
            part = jnp.dot(
                smooth[scale, :, 0:depth],
                table(scale, group, low, high),
                preferred_element_type=jnp.float32,
            )
            return part if first else part + total[scale, :, low:high]

        if not last:

            def scan_step(turn, carry):
                for scale in (turn * 2 + one for one in range(2)):
                    for low, high in columns:
                        total[scale, :, low:high] = part_of(scale, low, high)
                return carry

            lax.fori_loop(0, scales // 2, scan_step, 0)
            continue
        for low, high in columns:

            def last_step(turn, carry):
                peak, energy = best[:, low:high], power[:, low:high]
                for one in range(SCAN_UNROLL):
                    part = part_of(turn * SCAN_UNROLL + one, low, high)
                    peak = jnp.maximum(peak, part)
                    energy = energy + part * part
                best[:, low:high] = peak
                power[:, low:high] = energy
                return carry

            best[:, low:high] = jnp.full((rows, high - low), -jnp.inf, jnp.float32)
            power[:, low:high] = jnp.zeros((rows, high - low), jnp.float32)
            lax.fori_loop(0, scales // SCAN_UNROLL, last_step, 0)
            for tile in range(low // LANES, high // LANES):
                finish(tile)

    for tile in range(tiles):
        up, down = copies(tile)
        pl.when(has_high)(up.wait_send)
        pl.when(has_low)(down.wait_send)
    for store in stores:
        store.wait()


def per_device(slab, widths):
    frames, mz_bins, scans = slab.shape
    scales = widths.shape[0]
    strip = mz_bins // lax.axis_size("scale")
    tiles = scans // LANES
    rows = frames * strip
    bf16, f32 = jnp.bfloat16, jnp.float32
    edges = [0] + [edge for edge in EDGES if edge < tiles] + [tiles]
    depth = LANES * max(high - low for low, high in zip(edges, edges[1:]))
    flops = 2 * scales * rows * scans * (scans + 6 * frames)
    return pl.pallas_call(
        functools.partial(kernel, lax.axis_size("rt")),
        out_shape=(
            jax.ShapeDtypeStruct((frames, strip, scans), bf16),
            jax.ShapeDtypeStruct((frames, strip, scans), f32),
        ),
        in_specs=[
            pl.BlockSpec(memory_space=pltpu.SMEM),
            pl.BlockSpec(memory_space=pl.ANY),
        ],
        out_specs=(pl.BlockSpec(memory_space=pl.ANY), pl.BlockSpec(memory_space=pl.ANY)),
        scratch_shapes=[
            pltpu.VMEM((tiles, frames, strip, LANES), f32),
            pltpu.VMEM((tiles, strip // 2, 6 * frames, LANES), bf16),
            pltpu.VMEM((scales * 2 * frames, 6 * frames), bf16),
            pltpu.VMEM((scales, LANES, 2 * scans - LANES), bf16),
            pltpu.VMEM((scales, rows, depth), bf16),
            pltpu.VMEM((scales, rows, scans), f32),
            pltpu.VMEM((rows, scans), f32),
            pltpu.VMEM((rows, scans), f32),
            pltpu.VMEM((tiles, frames, strip, LANES), f32),
            pltpu.VMEM((tiles, frames, strip, LANES), bf16),
            pltpu.VMEM((tiles, frames, strip, LANES), f32),
            pltpu.SemaphoreType.DMA((tiles,)),
            pltpu.SemaphoreType.DMA((2, tiles)),
            pltpu.SemaphoreType.DMA((2, tiles)),
            pltpu.SemaphoreType.DMA((2, tiles)),
        ],
        compiler_params=pltpu.CompilerParams(
            collective_id=0, has_side_effects=True, vmem_limit_bytes=58 * 1024 * 1024
        ),
        cost_estimate=pl.CostEstimate(
            flops=flops, bytes_accessed=10 * rows * scans, transcendentals=0
        ),
        name="wavelets",
    )(widths, slab)


def solution(mesh):
    in_specs = (P("rt", None, None), P())
    out_specs = (P("rt", "scale", None), P("rt", "scale", None))
    return jax.shard_map(
        per_device, mesh=mesh, in_specs=in_specs, out_specs=out_specs, check_vma=False
    )
```
